32 devices in a mesh: pipe: 8 (over y, x, core), seq: 4 (over z).
Axes of the slice: x: 2, y: 2, z: 4, core: 2. Of those that a mesh axis runs over, the one named last changes fastest.
Arguments:
- layer_input: bfloat16 [8, 256, 2, 1536], P('pipe', 'seq'), may hold values from -1.5 to 1.5
- grad_out: bfloat16 [8, 256, 2, 1536], P('pipe', 'seq'), may hold values from -6 to 6
- queries: bfloat16 [8, 256, 2, 768], P('pipe', 'seq'), may hold values from -8 to 8
- keys_saved: bfloat16 [8, 256, 2, 768], P('pipe', 'seq'), may hold values from -8 to 8
- values_saved: bfloat16 [8, 256, 2, 768], P('pipe', 'seq'), may hold values from -6 to 6
- out_weight: bfloat16 [8, 768, 1536], P('pipe'), may hold values from -0.15625 to 0.15625
- qkv_weight: bfloat16 [8, 1536, 2304], P('pipe'), may hold values from -0.125 to 0.125
- ln_gain: bfloat16 [8, 1536], P('pipe'), may hold values from 0.099609375 to 1.8984375
- lengths: int32 [8, 2], P('pipe'), may hold values from 33 to 256
Outputs:
- passed: bfloat16 [8, 256, 2, 1536], P('pipe', 'seq')
The draws below stay inside these ranges and needn't reach their ends.
All inputs are finite; a program needn't handle non-finite values.
Results may differ from the reference program's by a relative error of at most 0.0063.
Values may be sent and summed in bfloat16 or wider, within the bound.
A program may use at most 64 MiB of HBM per device.

```python
import jax
import jax.numpy as jnp
from jax import lax

D = 1536
HEADS_W = 12
HD = 64
RECS = 2
INNER = 768
LEN = 256
SECTIONS = 8


def shared_projections(key):
    full_shape = (SECTIONS, LEN, RECS, INNER)
    query_vals = jnp.clip(1.5 * jax.random.normal(jax.random.fold_in(key, 1), full_shape, jnp.float32), -8.0, 8.0)
    key_vals = jnp.clip(1.5 * jax.random.normal(jax.random.fold_in(key, 2), full_shape, jnp.float32), -8.0, 8.0)
    return (query_vals, key_vals)


def draw_queries(key, part):
    return shared_projections(jax.random.fold_in(key, 11))[0].astype(jnp.bfloat16)


def draw_keys_saved(key, part):
    return shared_projections(jax.random.fold_in(key, 11))[1].astype(jnp.bfloat16)


def place_ends(entries, stream_key, low, largest):
    longest = entries.shape.index(max(entries.shape))
    spots = []
    for shift in (0, 1):
        where = [jax.random.randint(jax.random.fold_in(stream_key, axis), (), 0, length) for axis, length in enumerate(entries.shape)]
        where[longest] = (where[longest] + shift) % entries.shape[longest]
        spots.append(tuple(where))
    return entries.at[spots[0]].set(low).at[spots[1]].set(largest)


def shard_levels(stream_key, shape, split, low, largest):
    loudness, own = 1.0, jax.random.fold_in(stream_key, 6)
    for axis_at, blocks in split:
        steps = jnp.exp(jax.random.uniform(jax.random.fold_in(own, axis_at), (blocks,), jnp.float32, low / len(split), largest / len(split)))
        loudness = loudness * jnp.repeat(steps, shape[axis_at] // blocks).reshape([-1 if axis == axis_at else 1 for axis in range(len(shape))])
    return loudness


def bell_draw(stream_key, dims, deviation, most, pieces=(), kind=jnp.bfloat16):
    values = jax.random.normal(stream_key, dims, jnp.float32) * deviation
    if len(pieces) > 0:
        values = shard_levels(stream_key, dims, pieces, -0.22, 0.18) * values
    return jnp.clip(values, min=-most, max=most).astype(kind)


def setup_inputs(seed: int = 0) -> dict:
    streams_of = jax.random.split(jax.random.key(seed), 10)
    return {
        "layer_input": bell_draw(streams_of[0], (SECTIONS, LEN, RECS, D), 0.25, 1.5, ((0, 8), (1, 4))),
        "grad_out": bell_draw(streams_of[1], (SECTIONS, LEN, RECS, D), 1.0, 6.0, ((0, 8), (1, 4))),
        "queries": draw_queries(jax.random.fold_in(streams_of[9], 71), 0),
        "keys_saved": draw_keys_saved(jax.random.fold_in(streams_of[9], 71), 0),
        "values_saved": bell_draw(streams_of[4], (SECTIONS, LEN, RECS, INNER), 1.0, 6.0, ((0, 8), (1, 4))),
        "out_weight": bell_draw(streams_of[5], (SECTIONS, INNER, D), D ** -0.5, 0.15625, ((0, 8),)),
        "qkv_weight": bell_draw(streams_of[6], (SECTIONS, D, 3 * INNER), (3 * INNER) ** -0.5, 0.125, ((0, 8),)),
        "ln_gain": jnp.clip(1.0 + 0.18 * jax.random.normal(streams_of[7], (SECTIONS, D), jnp.float32), 0.099609375, 1.8984375).astype(jnp.bfloat16),
        "lengths": place_ends(jax.random.randint(streams_of[8], (SECTIONS, RECS), LEN // 8 + 1, LEN + 1), jax.random.fold_in(streams_of[8], 1), LEN // 8 + 1, LEN).astype(jnp.int32),
    }


def norm_backward(inputs, norm_gain, upstream):
    row_mean = lax.optimization_barrier(jnp.mean(inputs, axis=-1, keepdims=True))
    centred = inputs - row_mean
    row_var = lax.optimization_barrier(jnp.mean(centred * centred, axis=-1, keepdims=True))
    inv_std = lax.rsqrt(row_var + 1e-05)
    normed = centred * inv_std
    scaled = upstream * norm_gain
    return inv_std * (scaled - lax.optimization_barrier(jnp.mean(scaled, axis=-1, keepdims=True)) - normed * lax.optimization_barrier(jnp.mean(scaled * normed, axis=-1, keepdims=True)))

def one_pair(operands):
    query_rows, key_rows, value_rows, grad_rows, key_length = operands
    factor = HD ** (-0.5)
    scores = jnp.dot(query_rows, key_rows.T, preferred_element_type=jnp.float32) * factor
    usable = jnp.arange(LEN) < key_length
    masked = jnp.where(usable[None, :], scores, -jnp.inf)
    row_peak = lax.optimization_barrier(jnp.max(masked, axis=-1, keepdims=True))
    exp_terms = jnp.exp(masked - row_peak)
    prob_full = exp_terms / lax.optimization_barrier(jnp.sum(exp_terms, axis=-1, keepdims=True))
    prob_low = prob_full.astype(jnp.bfloat16)
    grad_value = jnp.dot(prob_low.T, grad_rows, preferred_element_type=jnp.float32).astype(jnp.bfloat16)
    grad_prob = jnp.dot(grad_rows, value_rows.T, preferred_element_type=jnp.float32)
    row_delta = lax.optimization_barrier(jnp.sum(prob_full * grad_prob, axis=-1, keepdims=True))
    grad_score = (prob_full * (grad_prob - row_delta)).astype(jnp.bfloat16)
    grad_query = (jnp.dot(grad_score, key_rows, preferred_element_type=jnp.float32) * factor).astype(jnp.bfloat16)
    grad_key = (jnp.dot(grad_score.T, query_rows, preferred_element_type=jnp.float32) * factor).astype(jnp.bfloat16)
    return (grad_query, grad_key, grad_value)

def section_backward(operands):
    layer_input, grad_out, queries, keys_saved, values_saved, out_weight, qkv_weight, ln_gain, lengths = operands
    row_count = LEN * RECS
    pair_count = RECS * HEADS_W
    flat_grad = grad_out.reshape(row_count, D)
    heads_grad = lax.dot_general(flat_grad, out_weight, (((1,), (1,)), ((), ())), preferred_element_type=jnp.float32).astype(jnp.bfloat16)

    def by_pair(matrix):
        return jnp.transpose(matrix.reshape(LEN, pair_count, HD), (1, 0, 2))
    key_lengths = jnp.repeat(lengths, HEADS_W)
    grad_query, grad_key, grad_value = lax.map(one_pair, (by_pair(queries), by_pair(keys_saved), by_pair(values_saved), by_pair(heads_grad), key_lengths))

    def by_frame(stacked):
        return jnp.transpose(stacked, (1, 0, 2)).reshape(row_count, INNER)
    joined = jnp.concatenate([by_frame(grad_query), by_frame(grad_key), by_frame(grad_value)], axis=1)
    grad_normed = lax.dot_general(joined, qkv_weight, (((1,), (1,)), ((), ())), preferred_element_type=jnp.float32)
    inputs = layer_input.reshape(row_count, D).astype(jnp.float32)
    branch = norm_backward(inputs, ln_gain.astype(jnp.float32)[None, :], grad_normed)
    total = flat_grad.astype(jnp.float32) + branch
    return total.astype(jnp.bfloat16).reshape(LEN, RECS, D)

def reference(layer_input, grad_out, queries, keys_saved, values_saved, out_weight, qkv_weight, ln_gain, lengths):
    grad_input = lax.map(section_backward, (layer_input, grad_out, queries, keys_saved, values_saved, out_weight, qkv_weight, ln_gain, lengths))
    return jnp.roll(grad_input, -1, axis=0)
```

```python
import functools

import jax
import jax.numpy as jnp
from jax import lax
from jax.experimental import pallas as pl
from jax.experimental.pallas import tpu as pltpu
from jax.sharding import PartitionSpec as P

HEADS_W = 12
HD = 64


def passed_along(block, axis, distance):
    devices = range(lax.axis_size(axis))
    route = [((i - distance) % len(devices), i) for i in devices]
    return lax.ppermute(block, axis, route)


def norm_backward(inputs, norm_gain, upstream):
    row_mean = jnp.mean(inputs, axis=-1, keepdims=True)
    centred = inputs - row_mean
    row_var = jnp.mean(centred * centred, axis=-1, keepdims=True)
    inv_std = lax.rsqrt(row_var + 1e-05)
    normed = centred * inv_std
    scaled = upstream * norm_gain
    return inv_std * (
        scaled
        - jnp.mean(scaled, axis=-1, keepdims=True)
        - normed * jnp.mean(scaled * normed, axis=-1, keepdims=True)
    )


def attend(query_heads, key_heads, value_heads, grad_heads, key_lengths):
    length = query_heads.shape[0]
    pair_count = query_heads.shape[1] // HD
    factor = HD ** (-0.5)
    query_split = query_heads.reshape(length, pair_count, HD)
    key_split = key_heads.reshape(length, pair_count, HD)
    value_split = value_heads.reshape(length, pair_count, HD)
    grad_split = grad_heads.reshape(length, pair_count, HD)
    block = 512 if length % 512 == 0 else length
    usable = jnp.arange(length)[None, None, :] < key_lengths[:, None, None]

    def one_block(carried, block_index):
        key_acc, value_acc = carried
        query_block = lax.dynamic_slice_in_dim(query_split, block_index * block, block, 0)
        grad_block = lax.dynamic_slice_in_dim(grad_split, block_index * block, block, 0)
        scores = (
            jnp.einsum("qph,kph->pqk", query_block, key_split, preferred_element_type=jnp.float32)
            * factor
        )
        masked = jnp.where(usable, scores, -jnp.inf)
        row_peak = jnp.max(masked, axis=-1, keepdims=True)
        exp_terms = jnp.exp(masked - row_peak)
        prob_full = exp_terms / jnp.sum(exp_terms, axis=-1, keepdims=True)
        prob_low = prob_full.astype(jnp.bfloat16)
        value_acc = value_acc + jnp.einsum(
            "pqk,qph->kph", prob_low, grad_block, preferred_element_type=jnp.float32
        )
        grad_prob = jnp.einsum(
            "qph,kph->pqk", grad_block, value_split, preferred_element_type=jnp.float32
        )
        row_delta = jnp.sum(prob_full * grad_prob, axis=-1, keepdims=True)
        grad_score = (prob_full * (grad_prob - row_delta)).astype(jnp.bfloat16)
        grad_query = (
            jnp.einsum("pqk,kph->qph", grad_score, key_split, preferred_element_type=jnp.float32)
            * factor
        ).astype(jnp.bfloat16)
        key_acc = key_acc + jnp.einsum(
            "pqk,qph->kph", grad_score, query_block, preferred_element_type=jnp.float32
        )
        return ((key_acc, value_acc), grad_query)

    empty_acc = jnp.zeros((length, pair_count, HD), jnp.float32)
    (key_acc, value_acc), query_blocks = lax.scan(
        one_block, (empty_acc, empty_acc), jnp.arange(length // block)
    )
    grad_query = query_blocks.reshape(length, pair_count * HD)
    grad_key = (key_acc * factor).astype(jnp.bfloat16).reshape(length, pair_count * HD)
    grad_value = value_acc.astype(jnp.bfloat16).reshape(length, pair_count * HD)
    return (grad_query, grad_key, grad_value)


def per_device(
    layer_input,
    grad_out,
    queries,
    keys_saved,
    values_saved,
    out_weight,
    qkv_weight,
    ln_gain,
    lengths,
):
    frames = grad_out.shape[1]
    record_count = grad_out.shape[2]
    feature_count = grad_out.shape[3]
    inner_width = out_weight.shape[1]
    row_count = frames * record_count
    flat_grad = grad_out[0].reshape(row_count, feature_count)
    query_cols = queries[0].reshape(frames, record_count * inner_width)
    key_cols = keys_saved[0].reshape(frames, record_count * inner_width)
    value_cols = values_saved[0].reshape(frames, record_count * inner_width)
    product = lax.dot_general(
        flat_grad, out_weight[0], (((1,), (1,)), ((), ())), preferred_element_type=jnp.float32
    )
    grad_cols = product.astype(jnp.bfloat16).reshape(frames, record_count * inner_width)
    query_heads, key_heads, value_heads, grad_heads = (
        lax.all_to_all(query_cols, "seq", split_axis=1, concat_axis=0, tiled=True),
        lax.all_to_all(key_cols, "seq", split_axis=1, concat_axis=0, tiled=True),
        lax.all_to_all(value_cols, "seq", split_axis=1, concat_axis=0, tiled=True),
        lax.all_to_all(grad_cols, "seq", split_axis=1, concat_axis=0, tiled=True),
    )
    pair_count = query_heads.shape[1] // HD
    pair_ids = lax.axis_index("seq") * pair_count + jnp.arange(pair_count)
    record_ids = pair_ids // HEADS_W
    key_lengths = jnp.sum(
        jnp.where(record_ids[:, None] == jnp.arange(record_count)[None, :], lengths[0][None, :], 0),
        axis=1,
    )
    grad_query, grad_key, grad_value = attend(
        query_heads, key_heads, value_heads, grad_heads, key_lengths
    )
    back_query, back_key, back_value = (
        lax.all_to_all(grad_query, "seq", split_axis=0, concat_axis=1, tiled=True),
        lax.all_to_all(grad_key, "seq", split_axis=0, concat_axis=1, tiled=True),
        lax.all_to_all(grad_value, "seq", split_axis=0, concat_axis=1, tiled=True),
    )
    joined = jnp.concatenate(
        [
            back_query.reshape(row_count, inner_width),
            back_key.reshape(row_count, inner_width),
            back_value.reshape(row_count, inner_width),
        ],
        axis=1,
    )
    grad_normed = lax.dot_general(
        joined, qkv_weight[0], (((1,), (1,)), ((), ())), preferred_element_type=jnp.float32
    )
    inputs = layer_input[0].reshape(row_count, feature_count).astype(jnp.float32)
    branch = norm_backward(inputs, ln_gain[0].astype(jnp.float32)[None, :], grad_normed)
    total = (flat_grad.astype(jnp.float32) + branch).astype(jnp.bfloat16)
    passed = passed_along(total, "pipe", -1)
    return passed.reshape(1, frames, record_count, feature_count)


UNIT = 2 * HD
NT = (((1,), (1,)), ((), ()))
TN = (((0,), (0,)), ((), ()))
NN = (((1,), (0,)), ((), ()))


def mm(lhs, rhs, dims):
    return lax.dot_general(lhs, rhs, dims, preferred_element_type=jnp.float32)


def unit_attention(q, k, v, g, key_length):
    length = q.shape[0]
    first = lax.broadcasted_iota(jnp.int32, (1, UNIT), 1) < HD
    usable = lax.broadcasted_iota(jnp.int32, (length, 1), 0) < key_length
    zero = jnp.zeros((), k.dtype)
    halves = []
    for head in range(2):
        k_head = jnp.where(first, k, zero) if head == 0 else jnp.where(first, zero, k)
        v_head = jnp.where(first, v, zero) if head == 0 else jnp.where(first, zero, v)
        scores = jnp.where(usable, mm(k_head, q, NT), -jnp.inf)
        terms = jnp.exp(scores - jnp.max(scores, axis=0, keepdims=True))
        prob = terms * (1.0 / jnp.sum(terms, axis=0, keepdims=True))
        grad_prob = mm(v_head, g, NT)
        delta = jnp.sum(prob * grad_prob, axis=0, keepdims=True)
        grad_score = (prob * (grad_prob - delta)).astype(jnp.bfloat16)
        halves.append((
            mm(grad_score, k, TN) * (HD ** -0.5),
            mm(grad_score, q, NN),
            mm(prob.astype(jnp.bfloat16), g, NN),
        ))
    return [jnp.where(first, a, b).astype(jnp.bfloat16) for a, b in zip(*halves)]


def fused_kernel(
    n, pipes, frames, recs, width, inner,
    lens, gain, q_h, k_h, v_h, go_h, ow_h, li_h, qw_h,
    out,
    q_v, k_v, v_v, go_v, ow_v, li_v, qw_v, g32, st, stg, rx, rxg, rs, jn, acc, normed, inv,
    o_send, o_recv, o32,
    load_sem, fs, fr, gs, gr, bs, br, ps, pr,
):
    seq, pipe = lax.axis_index("seq"), lax.axis_index("pipe")
    per_rec = inner // UNIT
    units = recs * per_rec
    phases = units // n
    length = n * frames

    loads = [
        pltpu.make_async_copy(src, dst, load_sem.at[i])
        for i, (src, dst) in enumerate(
            [(q_h, q_v), (k_h, k_v), (v_h, v_v), (go_h, go_v), (ow_h, ow_v), (li_h, li_v), (qw_h, qw_v)]
        )
    ]
    for load in loads:
        load.start()

    peers = [lax.rem(seq + off, n) for off in range(1, n)]
    before, after = lax.rem(pipe + pipes - 1, pipes), lax.rem(pipe + 1, pipes)
    barrier = pltpu.get_barrier_semaphore()
    for peer in peers:
        pl.semaphore_signal(barrier, inc=1, device_id=(pipe, peer), device_id_type=pl.DeviceIdType.MESH)
    for other in (before, after):
        pl.semaphore_signal(barrier, inc=1, device_id=(other, seq), device_id_type=pl.DeviceIdType.MESH)

    def send(src, dst, s_sem, r_sem, to):
        return pltpu.make_async_remote_copy(
            src_ref=src, dst_ref=dst, send_sem=s_sem, recv_sem=r_sem,
            device_id=to, device_id_type=pl.DeviceIdType.MESH,
        )

    def forward(p):
        return [
            send(st.at[p * n + d], rx.at[p, pl.ds(0, 3), seq], fs.at[p, i], fr.at[p, i], (pipe, d))
            for i, d in enumerate(peers)
        ]

    def forward_grad(p):
        return [
            send(stg.at[p * n + d], rxg.at[p, seq], gs.at[p, i], gr.at[p, i], (pipe, d))
            for i, d in enumerate(peers)
        ]

    def back(p):
        return [
            send(rs.at[p, d], jn.at[p * n + seq], bs.at[p, i], br.at[p, i], (pipe, d))
            for i, d in enumerate(peers)
        ]

    def along(r):
        return send(o_send.at[r], o_recv.at[r], ps.at[r], pr.at[r], (before, seq))

    def start(copies):
        for copy in copies:
            copy.start()

    for load in loads[:3]:
        load.wait()
    for t, src in enumerate((q_v, k_v, v_v)):
        for r in range(recs):
            rows = src[:, r, :]
            if t == 0:
                rows = rows * jnp.asarray(HD ** -0.5, rows.dtype)
            for j in range(per_rec):
                st[r * per_rec + j, t] = rows[:, j * UNIT : (j + 1) * UNIT]
    pl.semaphore_wait(barrier, n + 1)
    start(forward(0))

    loads[3].wait()
    loads[4].wait()
    product = mm(go_v[...].reshape(frames * recs, width), ow_v[...], NT)
    for j in range(per_rec):
        g32[j] = product[:, j * UNIT : (j + 1) * UNIT]
    for r in range(recs):
        for j in range(per_rec):
            rows = g32[j, pl.ds(r, frames, stride=recs), :]
            stg[r * per_rec + j] = rows.astype(jnp.bfloat16)
    start(forward_grad(0))
    for p in range(1, phases):
        start(forward(p))
        start(forward_grad(p))

    for p in range(phases):
        for t in range(3):
            rx[p, t, seq] = st[p * n + seq, t]
        rxg[p, seq] = stg[p * n + seq]

    loads[5].wait()
    for r in range(recs):
        inputs = li_v[:, r, :].astype(jnp.float32)
        centred = inputs - jnp.mean(inputs, axis=-1, keepdims=True)
        inv_std = lax.rsqrt(jnp.mean(centred * centred, axis=-1, keepdims=True) + 1e-05)
        normed[r] = centred * inv_std
        inv[r] = jnp.broadcast_to(inv_std, (frames, 128))

    def attention(p):
        for copy in forward(p) + forward_grad(p):
            copy.wait_recv()
        q, k, v = (rx[p, t].reshape(length, UNIT) for t in range(3))
        g = rxg[p].reshape(length, UNIT)
        rec = lax.div(p * n + seq, per_rec)
        key_length = lens[0]
        for r in range(1, recs):
            key_length = jnp.where(rec == r, lens[r], key_length)
        for t, grad in enumerate(unit_attention(q, k, v, g, key_length)):
            rs[p, :, t] = grad.reshape(n, frames, UNIT)
        start(back(p))
        for t in range(3):
            jn[p * n + seq, t] = rs[p, seq, t]

    def project(p):
        for copy in back(p):
            copy.wait_recv()
        for r in range(recs):
            low, high = max(p * n, r * per_rec), min((p + 1) * n, (r + 1) * per_rec)
            if low >= high:
                continue
            for t in range(3):
                block = jnp.concatenate([jn[u, t] for u in range(low, high)], axis=1)
                column = t * inner + (low - r * per_rec) * UNIT
                part = mm(block, qw_v[:, column : column + (high - low) * UNIT], NT)
                if low == r * per_rec and t == 0:
                    acc[r] = part
                else:
                    acc[r] += part
            if high == (r + 1) * per_rec:
                scaled = acc[r] * gain[...].astype(jnp.float32)
                rows = normed[r]
                branch = inv[r][:, :1] * (
                    scaled
                    - jnp.mean(scaled, axis=-1, keepdims=True)
                    - rows * jnp.mean(scaled * rows, axis=-1, keepdims=True)
                )
                o_send[r] = (go_v[:, r, :].astype(jnp.float32) + branch).astype(jnp.bfloat16)
                along(r).start()

    for p in range(phases):
        attention(p)
        if p == 1:
            loads[6].wait()
        if p >= 1:
            project(p - 1)
    if phases == 1:
        loads[6].wait()
    project(phases - 1)
    for r in range(recs):
        along(r).wait_recv()
        o32[:, r, :] = o_recv[r].astype(jnp.float32)
    out[...] = o32[...].astype(jnp.bfloat16)
    for p in range(phases):
        for copy in forward(p) + forward_grad(p) + back(p):
            copy.wait_send()
    for r in range(recs):
        along(r).wait_send()


def per_device_fused(
    layer_input, grad_out, queries, keys_saved, values_saved, out_weight, qkv_weight, ln_gain, lengths
):
    n, pipes = lax.axis_size("seq"), lax.axis_size("pipe")
    _, frames, recs, width = grad_out.shape
    inner = out_weight.shape[1]
    per_rec = inner // UNIT
    units = recs * per_rec
    phases = units // n
    bf16, f32 = jnp.bfloat16, jnp.float32
    vmem, hbm = pl.BlockSpec(memory_space=pltpu.VMEM), pl.BlockSpec(memory_space=pl.ANY)
    pairs = pltpu.SemaphoreType.DMA((phases, n - 1))
    scratch = [
        pltpu.VMEM((frames, recs, inner), bf16),
        pltpu.VMEM((frames, recs, inner), bf16),
        pltpu.VMEM((frames, recs, inner), bf16),
        pltpu.VMEM((frames, recs, width), bf16),
        pltpu.VMEM((inner, width), bf16),
        pltpu.VMEM((frames, recs, width), bf16),
        pltpu.VMEM((width, 3 * inner), bf16),
        pltpu.VMEM((per_rec, frames * recs, UNIT), f32),
        pltpu.VMEM((units, 3, frames, UNIT), bf16),
        pltpu.VMEM((units, frames, UNIT), bf16),
        pltpu.VMEM((phases, 3, n, frames, UNIT), bf16),
        pltpu.VMEM((phases, n, frames, UNIT), bf16),
        pltpu.VMEM((phases, n, 3, frames, UNIT), bf16),
        pltpu.VMEM((units, 3, frames, UNIT), bf16),
        pltpu.VMEM((recs, frames, width), f32),
        pltpu.VMEM((recs, frames, width), f32),
        pltpu.VMEM((recs, frames, 128), f32),
        pltpu.VMEM((recs, frames, width), bf16),
        pltpu.VMEM((recs, frames, width), bf16),
        pltpu.VMEM((frames, recs, width), f32),
        pltpu.SemaphoreType.DMA((7,)),
        pairs, pairs, pairs, pairs, pairs, pairs,
        pltpu.SemaphoreType.DMA((recs,)),
        pltpu.SemaphoreType.DMA((recs,)),
    ]
    passed = pl.pallas_call(
        functools.partial(fused_kernel, n, pipes, frames, recs, width, inner),
        out_shape=jax.ShapeDtypeStruct((frames, recs, width), bf16),
        in_specs=[pl.BlockSpec(memory_space=pltpu.SMEM), vmem] + [hbm] * 7,
        out_specs=vmem,
        scratch_shapes=scratch,
        compiler_params=pltpu.CompilerParams(
            collective_id=0, has_side_effects=True, vmem_limit_bytes=40 * 1024 * 1024
        ),
        cost_estimate=pl.CostEstimate(
            flops=8 * frames * recs * width * inner, bytes_accessed=8 * width * inner, transcendentals=0
        ),
    )(
        lengths[0], ln_gain, queries[0], keys_saved[0], values_saved[0], grad_out[0], out_weight[0],
        layer_input[0], qkv_weight[0],
    )
    return passed[None]


def body_for(
    layer_input, grad_out, queries, keys_saved, values_saved, out_weight, qkv_weight, ln_gain, lengths
):
    args = (
        layer_input, grad_out, queries, keys_saved, values_saved, out_weight, qkv_weight, ln_gain, lengths
    )
    n, pipes = lax.axis_size("seq"), lax.axis_size("pipe")
    _, frames, recs, _ = grad_out.shape
    inner = out_weight.shape[1]
    fits = (
        inner % UNIT == 0 and (recs * (inner // UNIT)) % n == 0 and n > 1 and pipes > 2
        and frames % 16 == 0 and n * frames <= 256 and recs == 2
    )
    return per_device_fused(*args) if fits else per_device(*args)


def solution(mesh):
    placed = (
        P("pipe", "seq", None, None),
        P("pipe", "seq", None, None),
        P("pipe", "seq", None, None),
        P("pipe", "seq", None, None),
        P("pipe", "seq", None, None),
        P("pipe", None, None),
        P("pipe", None, None),
        P("pipe", None),
        P("pipe", None),
    )
    return jax.shard_map(
        body_for,
        mesh=mesh,
        in_specs=placed,
        out_specs=P("pipe", "seq", None, None),
        check_vma=False,
    )
```

```python
import functools

import jax
import jax.numpy as jnp
from jax import lax
from jax.experimental import pallas as pl
from jax.experimental.pallas import tpu as pltpu
from jax.sharding import PartitionSpec as P

HEADS_W = 12
HD = 64


def passed_along(block, axis, distance):
    devices = range(lax.axis_size(axis))
    route = [((i - distance) % len(devices), i) for i in devices]
    return lax.ppermute(block, axis, route)


def norm_backward(inputs, norm_gain, upstream):
    row_mean = jnp.mean(inputs, axis=-1, keepdims=True)
    centred = inputs - row_mean
    row_var = jnp.mean(centred * centred, axis=-1, keepdims=True)
    inv_std = lax.rsqrt(row_var + 1e-05)
    normed = centred * inv_std
    scaled = upstream * norm_gain
    return inv_std * (
        scaled
        - jnp.mean(scaled, axis=-1, keepdims=True)
        - normed * jnp.mean(scaled * normed, axis=-1, keepdims=True)
    )


def attend(query_heads, key_heads, value_heads, grad_heads, key_lengths):
    length = query_heads.shape[0]
    pair_count = query_heads.shape[1] // HD
    factor = HD ** (-0.5)
    query_split = query_heads.reshape(length, pair_count, HD)
    key_split = key_heads.reshape(length, pair_count, HD)
    value_split = value_heads.reshape(length, pair_count, HD)
    grad_split = grad_heads.reshape(length, pair_count, HD)
    block = 512 if length % 512 == 0 else length
    usable = jnp.arange(length)[None, None, :] < key_lengths[:, None, None]

    def one_block(carried, block_index):
        key_acc, value_acc = carried
        query_block = lax.dynamic_slice_in_dim(query_split, block_index * block, block, 0)
        grad_block = lax.dynamic_slice_in_dim(grad_split, block_index * block, block, 0)
        scores = (
            jnp.einsum("qph,kph->pqk", query_block, key_split, preferred_element_type=jnp.float32)
            * factor
        )
        masked = jnp.where(usable, scores, -jnp.inf)
        row_peak = jnp.max(masked, axis=-1, keepdims=True)
        exp_terms = jnp.exp(masked - row_peak)
        prob_full = exp_terms / jnp.sum(exp_terms, axis=-1, keepdims=True)
        prob_low = prob_full.astype(jnp.bfloat16)
        value_acc = value_acc + jnp.einsum(
            "pqk,qph->kph", prob_low, grad_block, preferred_element_type=jnp.float32
        )
        grad_prob = jnp.einsum(
            "qph,kph->pqk", grad_block, value_split, preferred_element_type=jnp.float32
        )
        row_delta = jnp.sum(prob_full * grad_prob, axis=-1, keepdims=True)
        grad_score = (prob_full * (grad_prob - row_delta)).astype(jnp.bfloat16)
        grad_query = (
            jnp.einsum("pqk,kph->qph", grad_score, key_split, preferred_element_type=jnp.float32)
            * factor
        ).astype(jnp.bfloat16)
        key_acc = key_acc + jnp.einsum(
            "pqk,qph->kph", grad_score, query_block, preferred_element_type=jnp.float32
        )
        return ((key_acc, value_acc), grad_query)

    empty_acc = jnp.zeros((length, pair_count, HD), jnp.float32)
    (key_acc, value_acc), query_blocks = lax.scan(
        one_block, (empty_acc, empty_acc), jnp.arange(length // block)
    )
    grad_query = query_blocks.reshape(length, pair_count * HD)
    grad_key = (key_acc * factor).astype(jnp.bfloat16).reshape(length, pair_count * HD)
    grad_value = value_acc.astype(jnp.bfloat16).reshape(length, pair_count * HD)
    return (grad_query, grad_key, grad_value)


def per_device(
    layer_input,
    grad_out,
    queries,
    keys_saved,
    values_saved,
    out_weight,
    qkv_weight,
    ln_gain,
    lengths,
):
    frames = grad_out.shape[1]
    record_count = grad_out.shape[2]
    feature_count = grad_out.shape[3]
    inner_width = out_weight.shape[1]
    row_count = frames * record_count
    flat_grad = grad_out[0].reshape(row_count, feature_count)
    query_cols = queries[0].reshape(frames, record_count * inner_width)
    key_cols = keys_saved[0].reshape(frames, record_count * inner_width)
    value_cols = values_saved[0].reshape(frames, record_count * inner_width)
    product = lax.dot_general(
        flat_grad, out_weight[0], (((1,), (1,)), ((), ())), preferred_element_type=jnp.float32
    )
    grad_cols = product.astype(jnp.bfloat16).reshape(frames, record_count * inner_width)
    query_heads, key_heads, value_heads, grad_heads = (
        lax.all_to_all(query_cols, "seq", split_axis=1, concat_axis=0, tiled=True),
        lax.all_to_all(key_cols, "seq", split_axis=1, concat_axis=0, tiled=True),
        lax.all_to_all(value_cols, "seq", split_axis=1, concat_axis=0, tiled=True),
        lax.all_to_all(grad_cols, "seq", split_axis=1, concat_axis=0, tiled=True),
    )
    pair_count = query_heads.shape[1] // HD
    pair_ids = lax.axis_index("seq") * pair_count + jnp.arange(pair_count)
    record_ids = pair_ids // HEADS_W
    key_lengths = jnp.sum(
        jnp.where(record_ids[:, None] == jnp.arange(record_count)[None, :], lengths[0][None, :], 0),
        axis=1,
    )
    grad_query, grad_key, grad_value = attend(
        query_heads, key_heads, value_heads, grad_heads, key_lengths
    )
    back_query, back_key, back_value = (
        lax.all_to_all(grad_query, "seq", split_axis=0, concat_axis=1, tiled=True),
        lax.all_to_all(grad_key, "seq", split_axis=0, concat_axis=1, tiled=True),
        lax.all_to_all(grad_value, "seq", split_axis=0, concat_axis=1, tiled=True),
    )
    joined = jnp.concatenate(
        [
            back_query.reshape(row_count, inner_width),
            back_key.reshape(row_count, inner_width),
            back_value.reshape(row_count, inner_width),
        ],
        axis=1,
    )
    grad_normed = lax.dot_general(
        joined, qkv_weight[0], (((1,), (1,)), ((), ())), preferred_element_type=jnp.float32
    )
    inputs = layer_input[0].reshape(row_count, feature_count).astype(jnp.float32)
    branch = norm_backward(inputs, ln_gain[0].astype(jnp.float32)[None, :], grad_normed)
    total = (flat_grad.astype(jnp.float32) + branch).astype(jnp.bfloat16)
    passed = passed_along(total, "pipe", -1)
    return passed.reshape(1, frames, record_count, feature_count)


UNIT = 2 * HD
NT = (((1,), (1,)), ((), ()))
TN = (((0,), (0,)), ((), ()))
NN = (((1,), (0,)), ((), ()))


def mm(lhs, rhs, dims):
    return lax.dot_general(lhs, rhs, dims, preferred_element_type=jnp.float32)


def unit_attention(q, k, v, g, key_length):
    length = q.shape[0]
    first = lax.broadcasted_iota(jnp.int32, (1, UNIT), 1) < HD
    usable = lax.broadcasted_iota(jnp.int32, (length, 1), 0) < key_length
    zero = jnp.zeros((), k.dtype)
    halves = []
    for head in range(2):
        k_head = jnp.where(first, k, zero) if head == 0 else jnp.where(first, zero, k)
        v_head = jnp.where(first, v, zero) if head == 0 else jnp.where(first, zero, v)
        scores = jnp.where(usable, mm(k_head, q, NT), -jnp.inf)
        terms = jnp.exp(scores - jnp.max(scores, axis=0, keepdims=True))
        prob = terms * (1.0 / jnp.sum(terms, axis=0, keepdims=True))
        grad_prob = mm(v_head, g, NT)
        delta = jnp.sum(prob * grad_prob, axis=0, keepdims=True)
        grad_score = (prob * (grad_prob - delta)).astype(jnp.bfloat16)
        halves.append((
            mm(grad_score, k, TN) * (HD ** -0.5),
            mm(grad_score, q, NN),
            mm(prob.astype(jnp.bfloat16), g, NN),
        ))
    return [jnp.where(first, a, b).astype(jnp.bfloat16) for a, b in zip(*halves)]


def fused_kernel(
    n, pipes, frames, recs, width, inner,
    lens, gain, q_h, k_h, v_h, go_h, ow_h, li_h, qw_h,
    out,
    q_v, k_v, v_v, go_v, ow_v, li_v, qw_v, g32, st, stg, rx, rxg, rs, jn, acc, normed, inv,
    o_send, o_recv, o32,
    load_sem, fs, fr, gs, gr, bs, br, ps, pr,
):
    seq, pipe = lax.axis_index("seq"), lax.axis_index("pipe")
    per_rec = inner // UNIT
    units = recs * per_rec
    phases = units // n
    length = n * frames

    loads = [
        pltpu.make_async_copy(src, dst, load_sem.at[i])
        for i, (src, dst) in enumerate(
            [(q_h, q_v), (k_h, k_v), (v_h, v_v), (go_h, go_v), (ow_h, ow_v), (li_h, li_v), (qw_h, qw_v)]
        )
    ]
    for load in loads:
        load.start()

    peers = [lax.rem(seq + off, n) for off in range(1, n)]
    before, after = lax.rem(pipe + pipes - 1, pipes), lax.rem(pipe + 1, pipes)
    barrier = pltpu.get_barrier_semaphore()
    for peer in peers:
        pl.semaphore_signal(barrier, inc=1, device_id=(pipe, peer), device_id_type=pl.DeviceIdType.MESH)
    for other in (before, after):
        pl.semaphore_signal(barrier, inc=1, device_id=(other, seq), device_id_type=pl.DeviceIdType.MESH)

    def send(src, dst, s_sem, r_sem, to):
        return pltpu.make_async_remote_copy(
            src_ref=src, dst_ref=dst, send_sem=s_sem, recv_sem=r_sem,
            device_id=to, device_id_type=pl.DeviceIdType.MESH,
        )

    def forward(p):
        return [
            send(st.at[p * n + d], rx.at[p, pl.ds(0, 3), seq], fs.at[p, i], fr.at[p, i], (pipe, d))
            for i, d in enumerate(peers)
        ]

    def forward_grad(p):
        return [
            send(stg.at[p * n + d], rxg.at[p, seq], gs.at[p, i], gr.at[p, i], (pipe, d))
            for i, d in enumerate(peers)
        ]

    def back(p):
        return [
            send(rs.at[p, d], jn.at[p * n + seq], bs.at[p, i], br.at[p, i], (pipe, d))
            for i, d in enumerate(peers)
        ]

    def along(r):
        return send(o_send.at[r], o_recv.at[r], ps.at[r], pr.at[r], (before, seq))

    def start(copies):
        for copy in copies:
            copy.start()

    for load in loads[:3]:
        load.wait()
    for r in range(recs):
        for t, src in enumerate((q_v, k_v, v_v)):
            rows = src[:, r, :]
            if t == 0:
                rows = rows * jnp.asarray(HD ** -0.5, rows.dtype)
            for j in range(per_rec):
                st[r * per_rec + j, t] = rows[:, j * UNIT : (j + 1) * UNIT]
        if r == 0:
            pl.semaphore_wait(barrier, n + 1)
        if n <= (r + 1) * per_rec < n + per_rec:
            start(forward(0))

    loads[3].wait()
    loads[4].wait()
    product = mm(go_v[...].reshape(frames * recs, width), ow_v[...], NT)
    for j in range(per_rec):
        g32[j] = product[:, j * UNIT : (j + 1) * UNIT]
    for r in range(recs):
        for j in range(per_rec):
            rows = g32[j, pl.ds(r, frames, stride=recs), :]
            stg[r * per_rec + j] = rows.astype(jnp.bfloat16)
    start(forward_grad(0))
    if phases > 1:
        start(forward(1))
        start(forward_grad(1))

    for p in range(phases):
        for t in range(3):
            rx[p, t, seq] = st[p * n + seq, t]
        rxg[p, seq] = stg[p * n + seq]

    loads[5].wait()
    for r in range(recs):
        inputs = li_v[:, r, :].astype(jnp.float32)
        centred = inputs - jnp.mean(inputs, axis=-1, keepdims=True)
        inv_std = lax.rsqrt(jnp.mean(centred * centred, axis=-1, keepdims=True) + 1e-05)
        normed[r] = centred * inv_std
        inv[r] = jnp.broadcast_to(inv_std, (frames, 128))

    def attention(p):
        for copy in forward(p) + forward_grad(p):
            copy.wait_recv()
        if p + 2 < phases:
            start(forward(p + 2))
            start(forward_grad(p + 2))
        q, k, v = (rx[p, t].reshape(length, UNIT) for t in range(3))
        g = rxg[p].reshape(length, UNIT)
        rec = lax.div(p * n + seq, per_rec)
        key_length = lens[0]
        for r in range(1, recs):
            key_length = jnp.where(rec == r, lens[r], key_length)
        for t, grad in enumerate(unit_attention(q, k, v, g, key_length)):
            rs[p, :, t] = grad.reshape(n, frames, UNIT)
        start(back(p))
        for t in range(3):
            jn[p * n + seq, t] = rs[p, seq, t]

    def project(p):
        for copy in back(p):
            copy.wait_recv()
        for r in range(recs):
            low, high = max(p * n, r * per_rec), min((p + 1) * n, (r + 1) * per_rec)
            if low >= high:
                continue
            for t in range(3):
                block = jnp.concatenate([jn[u, t] for u in range(low, high)], axis=1)
                column = t * inner + (low - r * per_rec) * UNIT
                part = mm(block, qw_v[:, column : column + (high - low) * UNIT], NT)
                if low == r * per_rec and t == 0:
                    acc[r] = part
                else:
                    acc[r] += part
            if high == (r + 1) * per_rec:
                scaled = acc[r] * gain[...].astype(jnp.float32)
                rows = normed[r]
                branch = inv[r][:, :1] * (
                    scaled
                    - jnp.mean(scaled, axis=-1, keepdims=True)
                    - rows * jnp.mean(scaled * rows, axis=-1, keepdims=True)
                )
                o_send[r] = (go_v[:, r, :].astype(jnp.float32) + branch).astype(jnp.bfloat16)
                along(r).start()

    for p in range(phases):
        attention(p)
        if p == 1:
            loads[6].wait()
        if p >= 1:
            project(p - 1)
    if phases == 1:
        loads[6].wait()
    project(phases - 1)
    for r in range(recs):
        along(r).wait_recv()
        o32[:, r, :] = o_recv[r].astype(jnp.float32)
    out[...] = o32[...].astype(jnp.bfloat16)
    for p in range(phases):
        for copy in forward(p) + forward_grad(p) + back(p):
            copy.wait_send()
    for r in range(recs):
        along(r).wait_send()


def per_device_fused(
    layer_input, grad_out, queries, keys_saved, values_saved, out_weight, qkv_weight, ln_gain, lengths
):
    n, pipes = lax.axis_size("seq"), lax.axis_size("pipe")
    _, frames, recs, width = grad_out.shape
    inner = out_weight.shape[1]
    per_rec = inner // UNIT
    units = recs * per_rec
    phases = units // n
    bf16, f32 = jnp.bfloat16, jnp.float32
    vmem, hbm = pl.BlockSpec(memory_space=pltpu.VMEM), pl.BlockSpec(memory_space=pltpu.HBM)
    pairs = pltpu.SemaphoreType.DMA((phases, n - 1))
    scratch = [
        pltpu.VMEM((frames, recs, inner), bf16),
        pltpu.VMEM((frames, recs, inner), bf16),
        pltpu.VMEM((frames, recs, inner), bf16),
        pltpu.VMEM((frames, recs, width), bf16),
        pltpu.VMEM((inner, width), bf16),
        pltpu.VMEM((frames, recs, width), bf16),
        pltpu.VMEM((width, 3 * inner), bf16),
        pltpu.VMEM((per_rec, frames * recs, UNIT), f32),
        pltpu.VMEM((units, 3, frames, UNIT), bf16),
        pltpu.VMEM((units, frames, UNIT), bf16),
        pltpu.VMEM((phases, 3, n, frames, UNIT), bf16),
        pltpu.VMEM((phases, n, frames, UNIT), bf16),
        pltpu.VMEM((phases, n, 3, frames, UNIT), bf16),
        pltpu.VMEM((units, 3, frames, UNIT), bf16),
        pltpu.VMEM((recs, frames, width), f32),
        pltpu.VMEM((recs, frames, width), f32),
        pltpu.VMEM((recs, frames, 128), f32),
        pltpu.VMEM((recs, frames, width), bf16),
        pltpu.VMEM((recs, frames, width), bf16),
        pltpu.VMEM((frames, recs, width), f32),
        pltpu.SemaphoreType.DMA((7,)),
        pairs, pairs, pairs, pairs, pairs, pairs,
        pltpu.SemaphoreType.DMA((recs,)),
        pltpu.SemaphoreType.DMA((recs,)),
    ]
    passed = pl.pallas_call(
        functools.partial(fused_kernel, n, pipes, frames, recs, width, inner),
        out_shape=jax.ShapeDtypeStruct((frames, recs, width), bf16),
        in_specs=[pl.BlockSpec(memory_space=pltpu.SMEM), vmem] + [hbm] * 7,
        out_specs=vmem,
        scratch_shapes=scratch,
        compiler_params=pltpu.CompilerParams(
            collective_id=0, has_side_effects=True, vmem_limit_bytes=52 * 1024 * 1024
        ),
        cost_estimate=pl.CostEstimate(
            flops=8 * frames * recs * width * inner, bytes_accessed=8 * width * inner, transcendentals=0
        ),
    )(
        lengths[0], ln_gain, queries[0], keys_saved[0], values_saved[0], grad_out[0], out_weight[0],
        layer_input[0], qkv_weight[0],
    )
    return passed[None]


def body_for(
    layer_input, grad_out, queries, keys_saved, values_saved, out_weight, qkv_weight, ln_gain, lengths
):
    args = (
        layer_input, grad_out, queries, keys_saved, values_saved, out_weight, qkv_weight, ln_gain, lengths
    )
    n, pipes = lax.axis_size("seq"), lax.axis_size("pipe")
    _, frames, recs, _ = grad_out.shape
    inner = out_weight.shape[1]
    fits = (
        inner % UNIT == 0 and (recs * (inner // UNIT)) % n == 0 and n > 1 and pipes > 2
        and frames % 16 == 0 and n * frames <= 256 and recs == 2
    )
    return per_device_fused(*args) if fits else per_device(*args)


def solution(mesh):
    placed = (
        P("pipe", "seq", None, None),
        P("pipe", "seq", None, None),
        P("pipe", "seq", None, None),
        P("pipe", "seq", None, None),
        P("pipe", "seq", None, None),
        P("pipe", None, None),
        P("pipe", None, None),
        P("pipe", None),
        P("pipe", None),
    )
    return jax.shard_map(
        body_for,
        mesh=mesh,
        in_specs=placed,
        out_specs=P("pipe", "seq", None, None),
        check_vma=False,
    )
```

```python
import functools

import jax
import jax.numpy as jnp
from jax import lax
from jax.experimental import pallas as pl
from jax.experimental.pallas import tpu as pltpu
from jax.sharding import PartitionSpec as P

HEADS_W = 12
HD = 64


def passed_along(block, axis, distance):
    devices = range(lax.axis_size(axis))
    route = [((i - distance) % len(devices), i) for i in devices]
    return lax.ppermute(block, axis, route)


def norm_backward(inputs, norm_gain, upstream):
    row_mean = jnp.mean(inputs, axis=-1, keepdims=True)
    centred = inputs - row_mean
    row_var = jnp.mean(centred * centred, axis=-1, keepdims=True)
    inv_std = lax.rsqrt(row_var + 1e-05)
    normed = centred * inv_std
    scaled = upstream * norm_gain
    return inv_std * (
        scaled
        - jnp.mean(scaled, axis=-1, keepdims=True)
        - normed * jnp.mean(scaled * normed, axis=-1, keepdims=True)
    )


def attend(query_heads, key_heads, value_heads, grad_heads, key_lengths):
    length = query_heads.shape[0]
    pair_count = query_heads.shape[1] // HD
    factor = HD ** (-0.5)
    query_split = query_heads.reshape(length, pair_count, HD)
    key_split = key_heads.reshape(length, pair_count, HD)
    value_split = value_heads.reshape(length, pair_count, HD)
    grad_split = grad_heads.reshape(length, pair_count, HD)
    block = 512 if length % 512 == 0 else length
    usable = jnp.arange(length)[None, None, :] < key_lengths[:, None, None]

    def one_block(carried, block_index):
        key_acc, value_acc = carried
        query_block = lax.dynamic_slice_in_dim(query_split, block_index * block, block, 0)
        grad_block = lax.dynamic_slice_in_dim(grad_split, block_index * block, block, 0)
        scores = (
            jnp.einsum("qph,kph->pqk", query_block, key_split, preferred_element_type=jnp.float32)
            * factor
        )
        masked = jnp.where(usable, scores, -jnp.inf)
        row_peak = jnp.max(masked, axis=-1, keepdims=True)
        exp_terms = jnp.exp(masked - row_peak)
        prob_full = exp_terms / jnp.sum(exp_terms, axis=-1, keepdims=True)
        prob_low = prob_full.astype(jnp.bfloat16)
        value_acc = value_acc + jnp.einsum(
            "pqk,qph->kph", prob_low, grad_block, preferred_element_type=jnp.float32
        )
        grad_prob = jnp.einsum(
            "qph,kph->pqk", grad_block, value_split, preferred_element_type=jnp.float32
        )
        row_delta = jnp.sum(prob_full * grad_prob, axis=-1, keepdims=True)
        grad_score = (prob_full * (grad_prob - row_delta)).astype(jnp.bfloat16)
        grad_query = (
            jnp.einsum("pqk,kph->qph", grad_score, key_split, preferred_element_type=jnp.float32)
            * factor
        ).astype(jnp.bfloat16)
        key_acc = key_acc + jnp.einsum(
            "pqk,qph->kph", grad_score, query_block, preferred_element_type=jnp.float32
        )
        return ((key_acc, value_acc), grad_query)

    empty_acc = jnp.zeros((length, pair_count, HD), jnp.float32)
    (key_acc, value_acc), query_blocks = lax.scan(
        one_block, (empty_acc, empty_acc), jnp.arange(length // block)
    )
    grad_query = query_blocks.reshape(length, pair_count * HD)
    grad_key = (key_acc * factor).astype(jnp.bfloat16).reshape(length, pair_count * HD)
    grad_value = value_acc.astype(jnp.bfloat16).reshape(length, pair_count * HD)
    return (grad_query, grad_key, grad_value)


def per_device(
    layer_input,
    grad_out,
    queries,
    keys_saved,
    values_saved,
    out_weight,
    qkv_weight,
    ln_gain,
    lengths,
):
    frames = grad_out.shape[1]
    record_count = grad_out.shape[2]
    feature_count = grad_out.shape[3]
    inner_width = out_weight.shape[1]
    row_count = frames * record_count
    flat_grad = grad_out[0].reshape(row_count, feature_count)
    query_cols = queries[0].reshape(frames, record_count * inner_width)
    key_cols = keys_saved[0].reshape(frames, record_count * inner_width)
    value_cols = values_saved[0].reshape(frames, record_count * inner_width)
    product = lax.dot_general(
        flat_grad, out_weight[0], (((1,), (1,)), ((), ())), preferred_element_type=jnp.float32
    )
    grad_cols = product.astype(jnp.bfloat16).reshape(frames, record_count * inner_width)
    query_heads, key_heads, value_heads, grad_heads = (
        lax.all_to_all(query_cols, "seq", split_axis=1, concat_axis=0, tiled=True),
        lax.all_to_all(key_cols, "seq", split_axis=1, concat_axis=0, tiled=True),
        lax.all_to_all(value_cols, "seq", split_axis=1, concat_axis=0, tiled=True),
        lax.all_to_all(grad_cols, "seq", split_axis=1, concat_axis=0, tiled=True),
    )
    pair_count = query_heads.shape[1] // HD
    pair_ids = lax.axis_index("seq") * pair_count + jnp.arange(pair_count)
    record_ids = pair_ids // HEADS_W
    key_lengths = jnp.sum(
        jnp.where(record_ids[:, None] == jnp.arange(record_count)[None, :], lengths[0][None, :], 0),
        axis=1,
    )
    grad_query, grad_key, grad_value = attend(
        query_heads, key_heads, value_heads, grad_heads, key_lengths
    )
    back_query, back_key, back_value = (
        lax.all_to_all(grad_query, "seq", split_axis=0, concat_axis=1, tiled=True),
        lax.all_to_all(grad_key, "seq", split_axis=0, concat_axis=1, tiled=True),
        lax.all_to_all(grad_value, "seq", split_axis=0, concat_axis=1, tiled=True),
    )
    joined = jnp.concatenate(
        [
            back_query.reshape(row_count, inner_width),
            back_key.reshape(row_count, inner_width),
            back_value.reshape(row_count, inner_width),
        ],
        axis=1,
    )
    grad_normed = lax.dot_general(
        joined, qkv_weight[0], (((1,), (1,)), ((), ())), preferred_element_type=jnp.float32
    )
    inputs = layer_input[0].reshape(row_count, feature_count).astype(jnp.float32)
    branch = norm_backward(inputs, ln_gain[0].astype(jnp.float32)[None, :], grad_normed)
    total = (flat_grad.astype(jnp.float32) + branch).astype(jnp.bfloat16)
    passed = passed_along(total, "pipe", -1)
    return passed.reshape(1, frames, record_count, feature_count)


UNIT = 2 * HD
NT = (((1,), (1,)), ((), ()))
TN = (((0,), (0,)), ((), ()))
NN = (((1,), (0,)), ((), ()))


def mm(lhs, rhs, dims):
    return lax.dot_general(lhs, rhs, dims, preferred_element_type=jnp.float32)


def unit_attention(q, k, v, g, key_length):
    length = q.shape[0]
    first = lax.broadcasted_iota(jnp.int32, (1, UNIT), 1) < HD
    usable = lax.broadcasted_iota(jnp.int32, (length, 1), 0) < key_length
    zero = jnp.zeros((), k.dtype)
    halves = []
    for head in range(2):
        k_head = jnp.where(first, k, zero) if head == 0 else jnp.where(first, zero, k)
        v_head = jnp.where(first, v, zero) if head == 0 else jnp.where(first, zero, v)
        scores = jnp.where(usable, mm(k_head, q, NT), -jnp.inf)
        terms = jnp.exp(scores - jnp.max(scores, axis=0, keepdims=True))
        prob = terms * (1.0 / jnp.sum(terms, axis=0, keepdims=True))
        grad_prob = mm(v_head, g, NT)
        delta = jnp.sum(prob * grad_prob, axis=0, keepdims=True)
        grad_score = (prob * (grad_prob - delta)).astype(jnp.bfloat16)
        halves.append((
            mm(grad_score, k, TN) * (HD ** -0.5),
            mm(grad_score, q, NN),
            mm(prob.astype(jnp.bfloat16), g, NN),
        ))
    return [jnp.where(first, a, b).astype(jnp.bfloat16) for a, b in zip(*halves)]


def fused_kernel(
    n, pipes, frames, recs, width, inner,
    lens, gain, q_h, k_h, v_h, go_h, ow_h, li_h, qw_h,
    out,
    q_v, k_v, v_v, go_v, ow_v, li_v, qw_v, g32, st, stg, rx, rxg, rs, jn, acc, normed, inv,
    o_send, o_recv, o32,
    load_sem, fs, fr, gs, gr, bs, br, ps, pr,
):
    seq, pipe = lax.axis_index("seq"), lax.axis_index("pipe")
    per_rec = inner // UNIT
    units = recs * per_rec
    phases = units // n
    length = n * frames

    loads = [
        pltpu.make_async_copy(src, dst, load_sem.at[i])
        for i, (src, dst) in enumerate(
            [(q_h, q_v), (k_h, k_v), (v_h, v_v), (go_h, go_v), (ow_h, ow_v), (li_h, li_v), (qw_h, qw_v)]
        )
    ]
    for load in loads:
        load.start()

    peers = [lax.rem(seq + off, n) for off in range(1, n)]
    before, after = lax.rem(pipe + pipes - 1, pipes), lax.rem(pipe + 1, pipes)
    barrier = pltpu.get_barrier_semaphore()
    for peer in peers:
        pl.semaphore_signal(barrier, inc=1, device_id=(pipe, peer), device_id_type=pl.DeviceIdType.MESH)
    for other in (before, after):
        pl.semaphore_signal(barrier, inc=1, device_id=(other, seq), device_id_type=pl.DeviceIdType.MESH)

    def send(src, dst, s_sem, r_sem, to):
        return pltpu.make_async_remote_copy(
            src_ref=src, dst_ref=dst, send_sem=s_sem, recv_sem=r_sem,
            device_id=to, device_id_type=pl.DeviceIdType.MESH,
        )

    def forward(p):
        return [
            send(st.at[p * n + d], rx.at[p, pl.ds(0, 3), seq], fs.at[p, i], fr.at[p, i], (pipe, d))
            for i, d in enumerate(peers)
        ]

    def forward_grad(p):
        return [
            send(stg.at[p * n + d], rxg.at[p, seq], gs.at[p, i], gr.at[p, i], (pipe, d))
            for i, d in enumerate(peers)
        ]

    def pieces(p):
        count = 2 if p == phases - 1 else 1
        return [(i, pl.ds(i * (frames // count), frames // count)) for i in range(count)]

    def whole_at(r):
        return ((r + 1) * per_rec - 1) // n

    def back(p, part, rows):
        return [
            send(
                rs.at[p, d, pl.ds(0, 3), rows], jn.at[p * n + seq, pl.ds(0, 3), rows],
                bs.at[p, part, i], br.at[p, part, i], (pipe, d),
            )
            for i, d in enumerate(peers)
        ]

    def along(r, part, rows):
        return send(
            o_send.at[r, rows], o_recv.at[r, rows], ps.at[r, part], pr.at[r, part], (before, seq)
        )

    def start(copies):
        for copy in copies:
            copy.start()

    for load in loads[:3]:
        load.wait()
    for r in range(recs):
        for t, src in enumerate((q_v, k_v, v_v)):
            rows = src[:, r, :]
            if t == 0:
                rows = rows * jnp.asarray(HD ** -0.5, rows.dtype)
            for j in range(per_rec):
                st[r * per_rec + j, t] = rows[:, j * UNIT : (j + 1) * UNIT]
        if r == 0:
            pl.semaphore_wait(barrier, n + 1)
        if n <= (r + 1) * per_rec < n + per_rec:
            start(forward(0))

    loads[3].wait()
    loads[4].wait()
    product = mm(go_v[...].reshape(frames * recs, width), ow_v[...], NT)
    for j in range(per_rec):
        g32[j] = product[:, j * UNIT : (j + 1) * UNIT]
    for r in range(recs):
        for j in range(per_rec):
            rows = g32[j, pl.ds(r, frames, stride=recs), :]
            stg[r * per_rec + j] = rows.astype(jnp.bfloat16)
    start(forward_grad(0))
    if phases > 1:
        start(forward(1))
        start(forward_grad(1))

    for p in range(phases):
        for t in range(3):
            rx[p, t, seq] = st[p * n + seq, t]
        rxg[p, seq] = stg[p * n + seq]

    loads[5].wait()
    for r in range(recs):
        inputs = li_v[:, r, :].astype(jnp.float32)
        centred = inputs - jnp.mean(inputs, axis=-1, keepdims=True)
        inv_std = lax.rsqrt(jnp.mean(centred * centred, axis=-1, keepdims=True) + 1e-05)
        normed[r] = centred * inv_std
        inv[r] = jnp.broadcast_to(inv_std, (frames, 128))

    def attention(p):
        for copy in forward(p) + forward_grad(p):
            copy.wait_recv()
        if p + 2 < phases:
            start(forward(p + 2))
            start(forward_grad(p + 2))
        q, k, v = (rx[p, t].reshape(length, UNIT) for t in range(3))
        g = rxg[p].reshape(length, UNIT)
        rec = lax.div(p * n + seq, per_rec)
        key_length = lens[0]
        for r in range(1, recs):
            key_length = jnp.where(rec == r, lens[r], key_length)
        for t, grad in enumerate(unit_attention(q, k, v, g, key_length)):
            rs[p, :, t] = grad.reshape(n, frames, UNIT)
        for part, rows in pieces(p):
            start(back(p, part, rows))
        for t in range(3):
            jn[p * n + seq, t] = rs[p, seq, t]

    def project(p, part, rows):
        for copy in back(p, part, rows):
            copy.wait_recv()
        for r in range(recs):
            low, high = max(p * n, r * per_rec), min((p + 1) * n, (r + 1) * per_rec)
            if low >= high:
                continue
            total = None if low == r * per_rec else acc[r, rows]
            for t in range(3):
                block = jnp.concatenate([jn[u, t, rows] for u in range(low, high)], axis=1)
                column = t * inner + (low - r * per_rec) * UNIT
                term = mm(block, qw_v[:, column : column + (high - low) * UNIT], NT)
                total = term if total is None else total + term
            if p < whole_at(r):
                acc[r, rows] = total
            else:
                scaled = total * gain[...].astype(jnp.float32)
                unit = normed[r, rows]
                branch = inv[r, rows][:, :1] * (
                    scaled
                    - jnp.mean(scaled, axis=-1, keepdims=True)
                    - unit * jnp.mean(scaled * unit, axis=-1, keepdims=True)
                )
                o_send[r, rows] = (go_v[rows, r, :].astype(jnp.float32) + branch).astype(jnp.bfloat16)
                along(r, part, rows).start()

    for p in range(phases):
        attention(p)
    loads[6].wait()
    for p in range(phases):
        for part, rows in pieces(p):
            project(p, part, rows)
    for r in range(recs):
        for part, rows in pieces(whole_at(r)):
            along(r, part, rows).wait_recv()
            o32[rows, r, :] = o_recv[r, rows].astype(jnp.float32)
            if r == recs - 1:
                out[rows] = o32[rows].astype(jnp.bfloat16)
    for p in range(phases):
        for copy in forward(p) + forward_grad(p):
            copy.wait_send()
        for part, rows in pieces(p):
            for copy in back(p, part, rows):
                copy.wait_send()
    for r in range(recs):
        for part, rows in pieces(whole_at(r)):
            along(r, part, rows).wait_send()


def per_device_fused(
    layer_input, grad_out, queries, keys_saved, values_saved, out_weight, qkv_weight, ln_gain, lengths
):
    n, pipes = lax.axis_size("seq"), lax.axis_size("pipe")
    _, frames, recs, width = grad_out.shape
    inner = out_weight.shape[1]
    per_rec = inner // UNIT
    units = recs * per_rec
    phases = units // n
    bf16, f32 = jnp.bfloat16, jnp.float32
    vmem, hbm = pl.BlockSpec(memory_space=pltpu.VMEM), pl.BlockSpec(memory_space=pltpu.HBM)
    pairs = pltpu.SemaphoreType.DMA((phases, n - 1))
    scratch = [
        pltpu.VMEM((frames, recs, inner), bf16),
        pltpu.VMEM((frames, recs, inner), bf16),
        pltpu.VMEM((frames, recs, inner), bf16),
        pltpu.VMEM((frames, recs, width), bf16),
        pltpu.VMEM((inner, width), bf16),
        pltpu.VMEM((frames, recs, width), bf16),
        pltpu.VMEM((width, 3 * inner), bf16),
        pltpu.VMEM((per_rec, frames * recs, UNIT), f32),
        pltpu.VMEM((units, 3, frames, UNIT), bf16),
        pltpu.VMEM((units, frames, UNIT), bf16),
        pltpu.VMEM((phases, 3, n, frames, UNIT), bf16),
        pltpu.VMEM((phases, n, frames, UNIT), bf16),
        pltpu.VMEM((phases, n, 3, frames, UNIT), bf16),
        pltpu.VMEM((units, 3, frames, UNIT), bf16),
        pltpu.VMEM((recs, frames, width), f32),
        pltpu.VMEM((recs, frames, width), f32),
        pltpu.VMEM((recs, frames, 128), f32),
        pltpu.VMEM((recs, frames, width), bf16),
        pltpu.VMEM((recs, frames, width), bf16),
        pltpu.VMEM((frames, recs, width), f32),
        pltpu.SemaphoreType.DMA((7,)),
        pairs, pairs, pairs, pairs,
        pltpu.SemaphoreType.DMA((phases, 2, n - 1)),
        pltpu.SemaphoreType.DMA((phases, 2, n - 1)),
        pltpu.SemaphoreType.DMA((recs, 2)),
        pltpu.SemaphoreType.DMA((recs, 2)),
    ]
    passed = pl.pallas_call(
        functools.partial(fused_kernel, n, pipes, frames, recs, width, inner),
        out_shape=jax.ShapeDtypeStruct((frames, recs, width), bf16),
        in_specs=[pl.BlockSpec(memory_space=pltpu.SMEM), vmem] + [hbm] * 7,
        out_specs=vmem,
        scratch_shapes=scratch,
        compiler_params=pltpu.CompilerParams(
            collective_id=0, has_side_effects=True, vmem_limit_bytes=63 * 1024 * 1024
        ),
        cost_estimate=pl.CostEstimate(
            flops=8 * frames * recs * width * inner, bytes_accessed=8 * width * inner, transcendentals=0
        ),
    )(
        lengths[0], ln_gain, queries[0], keys_saved[0], values_saved[0], grad_out[0], out_weight[0],
        layer_input[0], qkv_weight[0],
    )
    return passed[None]


def body_for(
    layer_input, grad_out, queries, keys_saved, values_saved, out_weight, qkv_weight, ln_gain, lengths
):
    args = (
        layer_input, grad_out, queries, keys_saved, values_saved, out_weight, qkv_weight, ln_gain, lengths
    )
    n, pipes = lax.axis_size("seq"), lax.axis_size("pipe")
    _, frames, recs, _ = grad_out.shape
    inner = out_weight.shape[1]
    fits = (
        inner % UNIT == 0 and (recs * (inner // UNIT)) % n == 0 and n > 1 and pipes > 2
        and frames % 32 == 0 and n * frames <= 256 and recs == 2
    )
    return per_device_fused(*args) if fits else per_device(*args)


def solution(mesh):
    placed = (
        P("pipe", "seq", None, None),
        P("pipe", "seq", None, None),
        P("pipe", "seq", None, None),
        P("pipe", "seq", None, None),
        P("pipe", "seq", None, None),
        P("pipe", None, None),
        P("pipe", None, None),
        P("pipe", None),
        P("pipe", None),
    )
    return jax.shard_map(
        body_for,
        mesh=mesh,
        in_specs=placed,
        out_specs=P("pipe", "seq", None, None),
        check_vma=False,
    )
```

```python
import functools

import jax
import jax.numpy as jnp
from jax import lax
from jax.experimental import pallas as pl
from jax.experimental.pallas import tpu as pltpu
from jax.sharding import PartitionSpec as P

HEADS_W = 12
HD = 64


def passed_along(block, axis, distance):
    devices = range(lax.axis_size(axis))
    route = [((i - distance) % len(devices), i) for i in devices]
    return lax.ppermute(block, axis, route)


def norm_backward(inputs, norm_gain, upstream):
    row_mean = jnp.mean(inputs, axis=-1, keepdims=True)
    centred = inputs - row_mean
    row_var = jnp.mean(centred * centred, axis=-1, keepdims=True)
    inv_std = lax.rsqrt(row_var + 1e-05)
    normed = centred * inv_std
    scaled = upstream * norm_gain
    return inv_std * (
        scaled
        - jnp.mean(scaled, axis=-1, keepdims=True)
        - normed * jnp.mean(scaled * normed, axis=-1, keepdims=True)
    )


def attend(query_heads, key_heads, value_heads, grad_heads, key_lengths):
    length = query_heads.shape[0]
    pair_count = query_heads.shape[1] // HD
    factor = HD ** (-0.5)
    query_split = query_heads.reshape(length, pair_count, HD)
    key_split = key_heads.reshape(length, pair_count, HD)
    value_split = value_heads.reshape(length, pair_count, HD)
    grad_split = grad_heads.reshape(length, pair_count, HD)
    block = 512 if length % 512 == 0 else length
    usable = jnp.arange(length)[None, None, :] < key_lengths[:, None, None]

    def one_block(carried, block_index):
        key_acc, value_acc = carried
        query_block = lax.dynamic_slice_in_dim(query_split, block_index * block, block, 0)
        grad_block = lax.dynamic_slice_in_dim(grad_split, block_index * block, block, 0)
        scores = (
            jnp.einsum("qph,kph->pqk", query_block, key_split, preferred_element_type=jnp.float32)
            * factor
        )
        masked = jnp.where(usable, scores, -jnp.inf)
        row_peak = jnp.max(masked, axis=-1, keepdims=True)
        exp_terms = jnp.exp(masked - row_peak)
        prob_full = exp_terms / jnp.sum(exp_terms, axis=-1, keepdims=True)
        prob_low = prob_full.astype(jnp.bfloat16)
        value_acc = value_acc + jnp.einsum(
            "pqk,qph->kph", prob_low, grad_block, preferred_element_type=jnp.float32
        )
        grad_prob = jnp.einsum(
            "qph,kph->pqk", grad_block, value_split, preferred_element_type=jnp.float32
        )
        row_delta = jnp.sum(prob_full * grad_prob, axis=-1, keepdims=True)
        grad_score = (prob_full * (grad_prob - row_delta)).astype(jnp.bfloat16)
        grad_query = (
            jnp.einsum("pqk,kph->qph", grad_score, key_split, preferred_element_type=jnp.float32)
            * factor
        ).astype(jnp.bfloat16)
        key_acc = key_acc + jnp.einsum(
            "pqk,qph->kph", grad_score, query_block, preferred_element_type=jnp.float32
        )
        return ((key_acc, value_acc), grad_query)

    empty_acc = jnp.zeros((length, pair_count, HD), jnp.float32)
    (key_acc, value_acc), query_blocks = lax.scan(
        one_block, (empty_acc, empty_acc), jnp.arange(length // block)
    )
    grad_query = query_blocks.reshape(length, pair_count * HD)
    grad_key = (key_acc * factor).astype(jnp.bfloat16).reshape(length, pair_count * HD)
    grad_value = value_acc.astype(jnp.bfloat16).reshape(length, pair_count * HD)
    return (grad_query, grad_key, grad_value)


def per_device(
    layer_input,
    grad_out,
    queries,
    keys_saved,
    values_saved,
    out_weight,
    qkv_weight,
    ln_gain,
    lengths,
):
    frames = grad_out.shape[1]
    record_count = grad_out.shape[2]
    feature_count = grad_out.shape[3]
    inner_width = out_weight.shape[1]
    row_count = frames * record_count
    flat_grad = grad_out[0].reshape(row_count, feature_count)
    query_cols = queries[0].reshape(frames, record_count * inner_width)
    key_cols = keys_saved[0].reshape(frames, record_count * inner_width)
    value_cols = values_saved[0].reshape(frames, record_count * inner_width)
    product = lax.dot_general(
        flat_grad, out_weight[0], (((1,), (1,)), ((), ())), preferred_element_type=jnp.float32
    )
    grad_cols = product.astype(jnp.bfloat16).reshape(frames, record_count * inner_width)
    query_heads, key_heads, value_heads, grad_heads = (
        lax.all_to_all(query_cols, "seq", split_axis=1, concat_axis=0, tiled=True),
        lax.all_to_all(key_cols, "seq", split_axis=1, concat_axis=0, tiled=True),
        lax.all_to_all(value_cols, "seq", split_axis=1, concat_axis=0, tiled=True),
        lax.all_to_all(grad_cols, "seq", split_axis=1, concat_axis=0, tiled=True),
    )
    pair_count = query_heads.shape[1] // HD
    pair_ids = lax.axis_index("seq") * pair_count + jnp.arange(pair_count)
    record_ids = pair_ids // HEADS_W
    key_lengths = jnp.sum(
        jnp.where(record_ids[:, None] == jnp.arange(record_count)[None, :], lengths[0][None, :], 0),
        axis=1,
    )
    grad_query, grad_key, grad_value = attend(
        query_heads, key_heads, value_heads, grad_heads, key_lengths
    )
    back_query, back_key, back_value = (
        lax.all_to_all(grad_query, "seq", split_axis=0, concat_axis=1, tiled=True),
        lax.all_to_all(grad_key, "seq", split_axis=0, concat_axis=1, tiled=True),
        lax.all_to_all(grad_value, "seq", split_axis=0, concat_axis=1, tiled=True),
    )
    joined = jnp.concatenate(
        [
            back_query.reshape(row_count, inner_width),
            back_key.reshape(row_count, inner_width),
            back_value.reshape(row_count, inner_width),
        ],
        axis=1,
    )
    grad_normed = lax.dot_general(
        joined, qkv_weight[0], (((1,), (1,)), ((), ())), preferred_element_type=jnp.float32
    )
    inputs = layer_input[0].reshape(row_count, feature_count).astype(jnp.float32)
    branch = norm_backward(inputs, ln_gain[0].astype(jnp.float32)[None, :], grad_normed)
    total = (flat_grad.astype(jnp.float32) + branch).astype(jnp.bfloat16)
    passed = passed_along(total, "pipe", -1)
    return passed.reshape(1, frames, record_count, feature_count)


UNIT = 2 * HD
NT = (((1,), (1,)), ((), ()))
TN = (((0,), (0,)), ((), ()))
NN = (((1,), (0,)), ((), ()))


def mm(lhs, rhs, dims):
    return lax.dot_general(lhs, rhs, dims, preferred_element_type=jnp.float32)


def unit_attention(q, k, v, g, key_length):
    length = q.shape[0]
    first = lax.broadcasted_iota(jnp.int32, (1, UNIT), 1) < HD
    usable = lax.broadcasted_iota(jnp.int32, (length, 1), 0) < key_length
    zero = jnp.zeros((), k.dtype)
    halves = []
    for head in range(2):
        k_head = jnp.where(first, k, zero) if head == 0 else jnp.where(first, zero, k)
        v_head = jnp.where(first, v, zero) if head == 0 else jnp.where(first, zero, v)
        scores = jnp.where(usable, mm(k_head, q, NT), -jnp.inf)
        terms = jnp.exp(scores - jnp.max(scores, axis=0, keepdims=True))
        prob = terms * (1.0 / jnp.sum(terms, axis=0, keepdims=True))
        grad_prob = mm(v_head, g, NT)
        delta = jnp.sum(prob * grad_prob, axis=0, keepdims=True)
        grad_score = (prob * (grad_prob - delta)).astype(jnp.bfloat16)
        halves.append((
            mm(grad_score, k, TN) * (HD ** -0.5),
            mm(grad_score, q, NN),
            mm(prob.astype(jnp.bfloat16), g, NN),
        ))
    return [jnp.where(first, a, b).astype(jnp.bfloat16) for a, b in zip(*halves)]


def fused_kernel(
    n, pipes, frames, recs, width, inner,
    lens, gain, q_h, k_h, v_h, go_h, ow_h, li_h, qw_h,
    out,
    q_v, k_v, v_v, go_v, ow_v, li_v, qw_v, g32, st, stg, rx, rxg, rs, jn, acc, normed, inv,
    o_send,
    load_sem, fs, fr, gs, gr, bs, br, ps, pr,
):
    seq, pipe = lax.axis_index("seq"), lax.axis_index("pipe")
    per_rec = inner // UNIT
    units = recs * per_rec
    phases = units // n
    length = n * frames

    loads = [
        pltpu.make_async_copy(src, dst, load_sem.at[i])
        for i, (src, dst) in enumerate(
            [(q_h, q_v), (k_h, k_v), (v_h, v_v), (go_h, go_v), (ow_h, ow_v), (li_h, li_v), (qw_h, qw_v)]
        )
    ]
    for load in loads:
        load.start()

    peers = [lax.rem(seq + off, n) for off in range(1, n)]
    before, after = lax.rem(pipe + pipes - 1, pipes), lax.rem(pipe + 1, pipes)
    barrier = pltpu.get_barrier_semaphore()
    for peer in peers:
        pl.semaphore_signal(barrier, inc=1, device_id=(pipe, peer), device_id_type=pl.DeviceIdType.MESH)
    for other in (before, after):
        pl.semaphore_signal(barrier, inc=1, device_id=(other, seq), device_id_type=pl.DeviceIdType.MESH)

    def send(src, dst, s_sem, r_sem, to):
        return pltpu.make_async_remote_copy(
            src_ref=src, dst_ref=dst, send_sem=s_sem, recv_sem=r_sem,
            device_id=to, device_id_type=pl.DeviceIdType.MESH,
        )

    def forward(p):
        return [
            send(st.at[p * n + d], rx.at[p, pl.ds(0, 3), seq], fs.at[p, i], fr.at[p, i], (pipe, d))
            for i, d in enumerate(peers)
        ]

    def forward_grad(p):
        return [
            send(stg.at[p * n + d], rxg.at[p, seq], gs.at[p, i], gr.at[p, i], (pipe, d))
            for i, d in enumerate(peers)
        ]

    def pieces(p):
        count = 2 if p == phases - 1 else 1
        return [(i, pl.ds(i * (frames // count), frames // count)) for i in range(count)]

    def whole_at(r):
        return ((r + 1) * per_rec - 1) // n

    def back(p, part, rows):
        return [
            send(
                rs.at[p, d, pl.ds(0, 3), rows], jn.at[p * n + seq, pl.ds(0, 3), rows],
                bs.at[p, part, i], br.at[p, part, i], (pipe, d),
            )
            for i, d in enumerate(peers)
        ]

    def along(r, part, rows):
        return send(
            o_send.at[r, rows], out.at[r, rows], ps.at[r, part], pr.at[r, part], (before, seq)
        )

    def start(copies):
        for copy in copies:
            copy.start()

    for load in loads[:3]:
        load.wait()
    for r in range(recs):
        for t, src in enumerate((q_v, k_v, v_v)):
            rows = src[:, r, :]
            if t == 0:
                rows = rows * jnp.asarray(HD ** -0.5, rows.dtype)
            for j in range(per_rec):
                st[r * per_rec + j, t] = rows[:, j * UNIT : (j + 1) * UNIT]
        if r == 0:
            pl.semaphore_wait(barrier, n + 1)
        if n <= (r + 1) * per_rec < n + per_rec:
            start(forward(0))

    loads[3].wait()
    loads[4].wait()
    product = mm(go_v[...].reshape(frames * recs, width), ow_v[...], NT)
    for j in range(per_rec):
        g32[j] = product[:, j * UNIT : (j + 1) * UNIT]
    for r in range(recs):
        for j in range(per_rec):
            rows = g32[j, pl.ds(r, frames, stride=recs), :]
            stg[r * per_rec + j] = rows.astype(jnp.bfloat16)
    start(forward_grad(0))
    if phases > 1:
        start(forward(1))
        start(forward_grad(1))

    for p in range(phases):
        for t in range(3):
            rx[p, t, seq] = st[p * n + seq, t]
        rxg[p, seq] = stg[p * n + seq]

    loads[5].wait()
    for r in range(recs):
        inputs = li_v[:, r, :].astype(jnp.float32)
        centred = inputs - jnp.mean(inputs, axis=-1, keepdims=True)
        inv_std = lax.rsqrt(jnp.mean(centred * centred, axis=-1, keepdims=True) + 1e-05)
        normed[r] = centred * inv_std
        inv[r] = jnp.broadcast_to(inv_std, (frames, 128))

    def attention(p):
        for copy in forward(p) + forward_grad(p):
            copy.wait_recv()
        if p + 2 < phases:
            start(forward(p + 2))
            start(forward_grad(p + 2))
        q, k, v = (rx[p, t].reshape(length, UNIT) for t in range(3))
        g = rxg[p].reshape(length, UNIT)
        rec = lax.div(p * n + seq, per_rec)
        key_length = lens[0]
        for r in range(1, recs):
            key_length = jnp.where(rec == r, lens[r], key_length)
        for t, grad in enumerate(unit_attention(q, k, v, g, key_length)):
            rs[p, :, t] = grad.reshape(n, frames, UNIT)
        for part, rows in pieces(p):
            start(back(p, part, rows))
        for t in range(3):
            jn[p * n + seq, t] = rs[p, seq, t]

    def project(p, part, rows):
        for copy in back(p, part, rows):
            copy.wait_recv()
        for r in range(recs):
            low, high = max(p * n, r * per_rec), min((p + 1) * n, (r + 1) * per_rec)
            if low >= high:
                continue
            total = None if low == r * per_rec else acc[r, rows]
            for t in range(3):
                block = jnp.concatenate([jn[u, t, rows] for u in range(low, high)], axis=1)
                column = t * inner + (low - r * per_rec) * UNIT
                term = mm(block, qw_v[:, column : column + (high - low) * UNIT], NT)
                total = term if total is None else total + term
            if p < whole_at(r):
                acc[r, rows] = total
            else:
                scaled = total * gain[...].astype(jnp.float32)
                unit = normed[r, rows]
                branch = inv[r, rows][:, :1] * (
                    scaled
                    - jnp.mean(scaled, axis=-1, keepdims=True)
                    - unit * jnp.mean(scaled * unit, axis=-1, keepdims=True)
                )
                o_send[r, rows] = (go_v[rows, r, :].astype(jnp.float32) + branch).astype(jnp.bfloat16)
                along(r, part, rows).start()

    for p in range(phases):
        attention(p)
    loads[6].wait()
    for p in range(phases):
        for part, rows in pieces(p):
            project(p, part, rows)
    for r in range(recs):
        for part, rows in pieces(whole_at(r)):
            along(r, part, rows).wait_recv()
    for p in range(phases):
        for copy in forward(p) + forward_grad(p):
            copy.wait_send()
        for part, rows in pieces(p):
            for copy in back(p, part, rows):
                copy.wait_send()
    for r in range(recs):
        for part, rows in pieces(whole_at(r)):
            along(r, part, rows).wait_send()


def per_device_fused(
    layer_input, grad_out, queries, keys_saved, values_saved, out_weight, qkv_weight, ln_gain, lengths
):
    n, pipes = lax.axis_size("seq"), lax.axis_size("pipe")
    _, frames, recs, width = grad_out.shape
    inner = out_weight.shape[1]
    per_rec = inner // UNIT
    units = recs * per_rec
    phases = units // n
    bf16, f32 = jnp.bfloat16, jnp.float32
    vmem, hbm = pl.BlockSpec(memory_space=pltpu.VMEM), pl.BlockSpec(memory_space=pltpu.HBM)
    pairs = pltpu.SemaphoreType.DMA((phases, n - 1))
    scratch = [
        pltpu.VMEM((frames, recs, inner), bf16),
        pltpu.VMEM((frames, recs, inner), bf16),
        pltpu.VMEM((frames, recs, inner), bf16),
        pltpu.VMEM((frames, recs, width), bf16),
        pltpu.VMEM((inner, width), bf16),
        pltpu.VMEM((frames, recs, width), bf16),
        pltpu.VMEM((width, 3 * inner), bf16),
        pltpu.VMEM((per_rec, frames * recs, UNIT), f32),
        pltpu.VMEM((units, 3, frames, UNIT), bf16),
        pltpu.VMEM((units, frames, UNIT), bf16),
        pltpu.VMEM((phases, 3, n, frames, UNIT), bf16),
        pltpu.VMEM((phases, n, frames, UNIT), bf16),
        pltpu.VMEM((phases, n, 3, frames, UNIT), bf16),
        pltpu.VMEM((units, 3, frames, UNIT), bf16),
        pltpu.VMEM((recs, frames, width), f32),
        pltpu.VMEM((recs, frames, width), f32),
        pltpu.VMEM((recs, frames, 128), f32),
        pltpu.VMEM((recs, frames, width), bf16),
        pltpu.SemaphoreType.DMA((7,)),
        pairs, pairs, pairs, pairs,
        pltpu.SemaphoreType.DMA((phases, 2, n - 1)),
        pltpu.SemaphoreType.DMA((phases, 2, n - 1)),
        pltpu.SemaphoreType.DMA((recs, 2)),
        pltpu.SemaphoreType.DMA((recs, 2)),
    ]
    passed = pl.pallas_call(
        functools.partial(fused_kernel, n, pipes, frames, recs, width, inner),
        out_shape=jax.ShapeDtypeStruct((recs, frames, width), bf16),
        in_specs=[pl.BlockSpec(memory_space=pltpu.SMEM), vmem] + [hbm] * 7,
        out_specs=hbm,
        scratch_shapes=scratch,
        compiler_params=pltpu.CompilerParams(
            collective_id=0, has_side_effects=True, vmem_limit_bytes=63 * 1024 * 1024
        ),
        cost_estimate=pl.CostEstimate(
            flops=8 * frames * recs * width * inner, bytes_accessed=8 * width * inner, transcendentals=0
        ),
    )(
        lengths[0], ln_gain, queries[0], keys_saved[0], values_saved[0], grad_out[0], out_weight[0],
        layer_input[0], qkv_weight[0],
    )
    return jnp.transpose(passed, (1, 0, 2))[None]


def body_for(
    layer_input, grad_out, queries, keys_saved, values_saved, out_weight, qkv_weight, ln_gain, lengths
):
    args = (
        layer_input, grad_out, queries, keys_saved, values_saved, out_weight, qkv_weight, ln_gain, lengths
    )
    n, pipes = lax.axis_size("seq"), lax.axis_size("pipe")
    _, frames, recs, _ = grad_out.shape
    inner = out_weight.shape[1]
    fits = (
        inner % UNIT == 0 and (recs * (inner // UNIT)) % n == 0 and n > 1 and pipes > 2
        and frames % 32 == 0 and n * frames <= 256 and recs == 2
    )
    return per_device_fused(*args) if fits else per_device(*args)


def solution(mesh):
    placed = (
        P("pipe", "seq", None, None),
        P("pipe", "seq", None, None),
        P("pipe", "seq", None, None),
        P("pipe", "seq", None, None),
        P("pipe", "seq", None, None),
        P("pipe", None, None),
        P("pipe", None, None),
        P("pipe", None),
        P("pipe", None),
    )
    return jax.shard_map(
        body_for,
        mesh=mesh,
        in_specs=placed,
        out_specs=P("pipe", "seq", None, None),
        check_vma=False,
    )
```
